1024 devices in a mesh: comp: 16 (over z_hi, y, core), row: 64 (over z_lo, x).
Axes of the slice: x: 4, y: 4, z: 32 (z_hi: 2, z_lo: 16; z = z_hi * 16 + z_lo), core: 2. Of those that a mesh axis runs over, the one named last changes fastest.
Arguments:
- fourier: bfloat16 [2, 1024, 49152], P(None, 'comp', 'row'), may hold values from -6 to 6
- legendre: bfloat16 [1024, 1024, 1024], P(('comp', 'row')), may hold values from -5 to 5
- gauss_weight: float32 [1024], replicated, may hold values from 0.5 to 2
- kappa_spec: bfloat16 [48], replicated, may hold values from 1 to 16
- marine_tracer_fields: float32 [2, 4, 256, 8192], P(None, None, 'comp', 'row'), may hold values from -6 to 6
- kappa_h: float32 [4, 256, 8192], P(None, 'comp', 'row'), may hold values from 0.04 to 0.18
- kappa_v: float32 [4], replicated, may hold values from 0.02 to 0.12
- air_flux: bfloat16 [2, 64, 8192], P(None, 'comp', 'row'), may hold values from -6 to 6
- remap_weight: bfloat16 [64, 64, 2, 128, 128], P('comp', 'row'), may hold values from -0.375 to 0.375
- remap_source: int32 [64, 64, 2], P('comp', 'row'), may hold values from 0 to 255
Outputs:
- smoothed_harmonic_coefficients: bfloat16 [2, 1024, 49152], P(None, 'comp', 'row')
- ocean_out: float32 [2, 4, 256, 8192], P(None, None, 'comp', 'row')
- seawater_heat_on_aerial_grid: float32 [64, 8192], P('comp', 'row')
The draws below stay inside these ranges and needn't reach their ends.
Inputs may be any that keep to these rules, and one draw needn't show every extreme that they name: `remap_source`: entry (a, r, k) is the ocean row, within column band r, of the k-th source block of atmosphere block a.
All inputs are finite; a program needn't handle non-finite values.
Results may differ from the reference program's by a relative error of at most 0.0055.
Values may be sent and summed in bfloat16 or wider, within the bound.
A program may use at most 32 MiB of HBM per device.

```python
import math
from functools import partial
import jax
import jax.numpy as jnp
from jax import lax

LEV = 8
FIELDS = 3
C = 48
NHALF = 1024
M = 1024
NS = 1024
LEVO = 4
TRACERS = 2
FLUXES = 2
SEA_SITES_STRIP = 128
NSTEP = 4
KB = 2
SEA_LINE_TALLY = 256
OX = 8192
SKIN_TILE_TALLY = 64
N_ROW = 64


def set_ends(values, rng, least, high):
    extent = values.shape
    spot = [jax.random.randint(jax.random.fold_in(rng, axis), (), 0, extent[axis]) for axis in range(len(extent))]
    values = values.at[tuple(spot)].set(least)
    longest = extent.index(max(extent))
    spot[longest] = (spot[longest] + 1) % extent[longest]
    return values.at[tuple(spot)].set(high)


def levels(own_key, shape, split, smallest, largest):
    gain, own = 1.0, jax.random.fold_in(own_key, 6)
    for dim, shards_of in split:
        steps = jnp.exp(jax.random.uniform(jax.random.fold_in(own, dim), (shards_of,), jnp.float32, smallest / len(split), largest / len(split)))
        gain = gain * jnp.repeat(steps, shape[dim] // shards_of).reshape([-1 if axis == dim else 1 for axis in range(len(shape))])
    return gain


def gaussian(key, shape, spread, bound, shards=(), kind=jnp.bfloat16):
    level = levels(key, shape, shards, -0.22, 0.18) if shards else 1.0
    result = jax.random.normal(key, shape, jnp.float32) * spread * level
    return jnp.minimum(jnp.maximum(result, -bound), bound).astype(kind)


def setup_inputs(seed: int = 0) -> dict:
    seeds = jax.random.split(jax.random.key(seed), 11)
    return {
        "fourier": gaussian(seeds[0], (2, M, NHALF * C), 1.0, 6.0, ((1, 16), (2, 64))),
        "legendre": gaussian(seeds[1], (M, NHALF, NS), 1.0, 5.0, ((0, 1024),)),
        "gauss_weight": jnp.clip(jnp.exp(jax.random.uniform(seeds[2], (NHALF,), jnp.float32, math.log(0.5), math.log(2.0))), 0.5, 2.0),
        "kappa_spec": jnp.clip(jnp.exp(jax.random.uniform(seeds[3], (C,), jnp.float32, math.log(1.0), math.log(16.0))), 1.0, 16.0).astype(jnp.bfloat16),
        "marine_tracer_fields": gaussian(seeds[4], (TRACERS, LEVO, SEA_LINE_TALLY, OX), 1.0, 6.0, ((2, 16), (3, 64)), jnp.float32),
        "kappa_h": jnp.clip(jnp.exp(math.log(0.18) - 1.50407746 * jax.random.uniform(seeds[5], (LEVO, SEA_LINE_TALLY, OX), jnp.float32) ** levels(seeds[5], (LEVO, SEA_LINE_TALLY, OX), ((1, 16), (2, 64)), -0.2, 0.2)), 0.04, 0.18),
        "kappa_v": jnp.clip(jnp.exp(jax.random.uniform(seeds[6], (LEVO,), jnp.float32, math.log(0.02), math.log(0.12))), 0.02, 0.12),
        "air_flux": gaussian(seeds[7], (FLUXES, SKIN_TILE_TALLY, OX), 1.0, 6.0, ((1, 16), (2, 64))),
        "remap_weight": gaussian(seeds[8], (SKIN_TILE_TALLY, N_ROW, KB, SEA_SITES_STRIP, SEA_SITES_STRIP), (KB * SEA_SITES_STRIP) ** -0.5, 0.375, ((0, 16), (1, 64))),
        "remap_source": set_ends(jax.random.randint(seeds[9], (SKIN_TILE_TALLY, N_ROW, KB), 0, SEA_LINE_TALLY), jax.random.fold_in(seeds[9], 1), 0, SEA_LINE_TALLY - 1).astype(jnp.int32),
    }


def spectral_filter(coeffs, degrees, kappa_spec, top_degree):
    ratio = degrees * (degrees + 1.0) / (top_degree * (top_degree + 1.0))
    factor = 1.0 / (1.0 + kappa_spec.astype(jnp.float32)[None, :] * (ratio * ratio)[:, None])
    return (coeffs * factor).astype(jnp.bfloat16)


def transform_one(inputs, gauss_weight, kappa_spec):
    halves, legendre_rows, wave = inputs
    northern = halves[0].astype(jnp.float32)
    southern = halves[1].astype(jnp.float32)
    weights = gauss_weight[:, None]
    even_part = (weights * (northern + southern)).astype(jnp.bfloat16)
    odd_part = (weights * (northern - southern)).astype(jnp.bfloat16)
    half_width = NS // 2
    even_rows = legendre_rows[:, :half_width]
    odd_rows = legendre_rows[:, half_width:]
    top_degree = M + NS - 1
    degrees = 2 * jnp.arange(half_width, dtype=jnp.int32) + wave
    dims = (((0,), (0,)), ((), ()))
    even_spec = lax.dot_general(even_rows, even_part, dims, preferred_element_type=jnp.float32) / NHALF
    odd_spec = lax.dot_general(odd_rows, odd_part, dims, preferred_element_type=jnp.float32) / NHALF
    even_filt = spectral_filter(even_spec, degrees.astype(jnp.float32), kappa_spec, top_degree)
    odd_filt = spectral_filter(odd_spec, (degrees + 1).astype(jnp.float32), kappa_spec, top_degree)
    even_grid = jnp.dot(even_rows, even_filt, preferred_element_type=jnp.float32)
    odd_grid = jnp.dot(odd_rows, odd_filt, preferred_element_type=jnp.float32)
    return jnp.stack([even_grid + odd_grid, even_grid - odd_grid]).astype(jnp.bfloat16)


def ocean_step(climate_snapshot, kappa_h, kappa_v, open_up, open_down):
    upward = jnp.roll(climate_snapshot, 1, axis=2)
    downward = jnp.roll(climate_snapshot, -1, axis=2)
    western = jnp.roll(climate_snapshot, 1, axis=3)
    eastern = jnp.roll(climate_snapshot, -1, axis=3)
    lateral = (upward - climate_snapshot) * open_up + (downward - climate_snapshot) * open_down + (eastern - climate_snapshot) + (western - climate_snapshot)
    above = jnp.concatenate([climate_snapshot[:, :1], climate_snapshot[:, :-1]], axis=1)
    beneath = jnp.concatenate([climate_snapshot[:, 1:], climate_snapshot[:, -1:]], axis=1)
    vertical = above + beneath - 2.0 * climate_snapshot
    return climate_snapshot + kappa_h * lateral + kappa_v[:, None, None] * vertical


def reference(fourier, legendre, gauss_weight, kappa_spec, marine_tracer_fields, kappa_h, kappa_v, air_flux, remap_weight, remap_source):
    width = 2 * LEV * FIELDS
    blocks = jnp.swapaxes(fourier.reshape(2, M, NHALF, width), 0, 1)
    waves = jnp.arange(M, dtype=jnp.int32)
    mapped = lax.map(partial(transform_one, gauss_weight=gauss_weight, kappa_spec=kappa_spec), (blocks, legendre, waves))
    smoothed_harmonic_coefficients = jnp.swapaxes(mapped, 0, 1).reshape(2, M, NHALF * width)

    topmost_seawater_warmth = marine_tracer_fields[0, 0].astype(jnp.bfloat16)
    meridian_indices = jnp.transpose(topmost_seawater_warmth.reshape(SEA_LINE_TALLY, N_ROW, SEA_SITES_STRIP), (1, 0, 2))
    band_index = jnp.arange(N_ROW, dtype=jnp.int32)[None, :, None]
    picked_nonzeros = meridian_indices[band_index, remap_source]
    expanded_coupling_factors = remap_weight.astype(jnp.float32)
    seawater_heat_on_aerial_grid = jnp.einsum("oumy,oumyx->oux", picked_nonzeros.astype(jnp.float32), expanded_coupling_factors, precision=lax.Precision.HIGHEST)
    seawater_heat_on_aerial_grid = seawater_heat_on_aerial_grid.reshape(SKIN_TILE_TALLY, N_ROW * SEA_SITES_STRIP)

    flux_wide = air_flux.astype(jnp.float32).reshape(FLUXES, SKIN_TILE_TALLY, N_ROW, SEA_SITES_STRIP)
    contrib = jnp.einsum("farx,arkox->arkfo", flux_wide, expanded_coupling_factors, precision=lax.Precision.HIGHEST)
    targets = (band_index * SEA_LINE_TALLY + remap_source).astype(jnp.int32).reshape(-1)
    summed = jax.ops.segment_sum(contrib.reshape(-1, FLUXES, SEA_SITES_STRIP), targets, num_segments=N_ROW * SEA_LINE_TALLY)
    forcing = jnp.transpose(summed.reshape(N_ROW, SEA_LINE_TALLY, FLUXES, SEA_SITES_STRIP), (2, 1, 0, 3)).reshape(FLUXES, SEA_LINE_TALLY, OX)

    climate_snapshot = marine_tracer_fields.at[:, 0].add(forcing)
    rows_global = jnp.arange(SEA_LINE_TALLY, dtype=jnp.int32)
    open_up = (rows_global != 0).astype(jnp.float32)[:, None]
    open_down = (rows_global != SEA_LINE_TALLY - 1).astype(jnp.float32)[:, None]
    for section in range(NSTEP):
        climate_snapshot = ocean_step(climate_snapshot, kappa_h, kappa_v, open_up, open_down)
    return smoothed_harmonic_coefficients, climate_snapshot, seawater_heat_on_aerial_grid
```

```python
import functools

import jax
import jax.numpy as jnp
from jax import lax
from jax.experimental import pallas as pl
from jax.experimental.pallas import tpu as pltpu
from jax.sharding import PartitionSpec as P

NSTEP = 4
MESH = pl.DeviceIdType.MESH
BF = jnp.bfloat16
F32 = jnp.float32
NN = (((1,), (0,)), ((), ()))
NT = (((1,), (1,)), ((), ()))
TN = (((0,), (0,)), ((), ()))


def dot(a, b, dims=NN):
    return lax.dot_general(a, b, dims, preferred_element_type=F32)


def iota(shape, axis):
    return lax.broadcasted_iota(jnp.int32, shape, axis)


def wait_bytes(ref, sem):
    pltpu.make_async_copy(ref, ref, sem).wait()


def kernel(
    four, leg_hbm, gauss, kappa, fields, kap_h, kap_v, flux, wts_hbm, srcs,
    out_spec, out_ocean, out_heat,
    leg, wts, perm_leg, send1, recv1, send2, gath, nspack, nsrecv, ewpack, ewrecv,
    loc_sem, send_sem, recv_sem,
):
    rows = lax.axis_size("row")
    comps = lax.axis_size("comp")
    me = lax.axis_index("row")
    comp = lax.axis_index("comp")
    half = comps // 2
    zhi = comp // half
    inner = lax.rem(comp, half)
    partner = lax.rem(comp + half, comps)
    north = lax.rem(comp + comps - 1, comps)
    south = lax.rem(comp + 1, comps)
    west = lax.rem(me + rows - 1, rows)
    east = lax.rem(me + 1, rows)

    load_leg = pltpu.make_async_copy(leg_hbm, leg, loc_sem.at[0])
    load_leg.start()
    load_wts = pltpu.make_async_copy(wts_hbm, wts, loc_sem.at[1])
    load_wts.start()

    barrier = pltpu.get_barrier_semaphore()

    def greet_row(k, _):
        target = lax.rem(me + k, rows)
        pl.semaphore_signal(barrier, inc=1, device_id={"row": target}, device_id_type=MESH)
        return 0

    def greet_comp(k, _):
        target = lax.rem(comp + k, comps)
        pl.semaphore_signal(barrier, inc=1, device_id={"comp": target}, device_id_type=MESH)
        return 0

    lax.fori_loop(1, rows, greet_row, 0)
    lax.fori_loop(1, comps, greet_comp, 0)

    wide = four.shape[2]
    cols = kappa.shape[1]
    lats = wide // cols
    mid = wide // 2
    lane_lat = iota((1, wide), 1) // cols
    weight = jnp.zeros((1, wide), F32)
    for l in range(lats):
        weight = jnp.where(lane_lat == l, gauss[me * lats + l], weight)
    n = four[0].astype(F32)
    s = four[1].astype(F32)
    even = (weight * (n + s)).astype(BF)
    odd = (weight * (n - s)).astype(BF)
    first = jnp.concatenate([even[:, :mid], odd[:, :mid]], axis=1)
    second = jnp.concatenate([even[:, mid:], odd[:, mid:]], axis=1)
    send1[:, 0, :] = first
    send1[:, 1, :] = second

    pl.semaphore_wait(barrier, rows + comps - 2)

    def send_forward(k, _):
        target = lax.rem(me + k, rows)
        pltpu.make_async_remote_copy(
            src_ref=send1.at[target], dst_ref=recv1.at[me], send_sem=send_sem.at[0], recv_sem=recv_sem.at[0],
            device_id={"row": target}, device_id_type=MESH).start()
        return 0

    lax.fori_loop(1, rows, send_forward, 0)
    own1 = pltpu.make_async_copy(send1.at[me], recv1.at[me], loc_sem.at[2])
    own1.start()

    load_wts.wait()
    tile = fields.shape[2]
    cells = fields.shape[3]
    blocks = wts.shape[0]
    kb = srcs.shape[0]
    row16 = iota((16, cells), 0)
    lane16 = iota((16, cells), 1)
    rep = jnp.zeros((16, cells), F32)
    for f in range(2):
        for j in range(blocks):
            rep = jnp.where(row16 == f * blocks + j, flux[f, j // kb, :].astype(F32)[None, :], rep)
    contrib = jnp.zeros((16, cells), F32)
    for j in range(blocks):
        only = jnp.where(lax.rem(row16, blocks) == j, rep, 0.0).astype(BF)
        contrib = contrib + dot(only, wts[j], NT)
    src_row = jnp.zeros((16, cells), F32)
    for j in range(blocks):
        hit = (lane16 // 16 == inner) & (lax.rem(lane16, blocks) == j) & (row16 == zhi)
        src_row = jnp.where(hit, srcs[j % kb, j // kb].astype(F32), src_row)
    gath[comp, 0:16, :] = fields[0, 0].astype(BF)
    gath[comp, 16:32, :] = contrib.astype(BF)
    gath[comp, 32:48, :] = src_row.astype(BF)
    across = pltpu.make_async_remote_copy(
        src_ref=gath.at[comp], dst_ref=gath.at[comp], send_sem=send_sem.at[1], recv_sem=recv_sem.at[1],
        device_id={"comp": partner}, device_id_type=MESH)
    across.start()

    def send_inner(slot, which):
        def step(k, _):
            target = zhi * half + lax.rem(inner + k, half)
            pltpu.make_async_remote_copy(
                src_ref=gath.at[slot], dst_ref=gath.at[slot], send_sem=send_sem.at[which], recv_sem=recv_sem.at[which],
                device_id={"comp": target}, device_id_type=MESH).start()
            return 0

        lax.fori_loop(1, half, step, 0)

    send_inner(comp, 2)

    slabs = [fields[t, k] for t in range(2) for k in range(4)] + [kap_h[k] for k in range(4)]
    count = len(slabs)
    row8 = iota((8, cells), 0)
    for p in range(count // 2):
        a, b = slabs[2 * p], slabs[2 * p + 1]
        nspack[0, p] = jnp.where(row8 < 4, a[:8], pltpu.roll(b[:8], 4, 0))
        nspack[1, p] = jnp.where(row8 >= 4, a[tile - 8 :], pltpu.roll(b[tile - 8 :], 4, 0))
    to_north = pltpu.make_async_remote_copy(
        src_ref=nspack.at[0], dst_ref=nsrecv.at[0], send_sem=send_sem.at[4], recv_sem=recv_sem.at[4],
        device_id={"comp": north}, device_id_type=MESH)
    to_south = pltpu.make_async_remote_copy(
        src_ref=nspack.at[1], dst_ref=nsrecv.at[1], send_sem=send_sem.at[5], recv_sem=recv_sem.at[5],
        device_id={"comp": south}, device_id_type=MESH)
    to_north.start()
    to_south.start()

    load_leg.wait()
    nlat = leg.shape[0]
    group = 2 * rows
    gi = iota((256, 256), 0)
    pick = (iota((256, 256), 1) == 8 * lax.rem(gi, 32) + gi // 32).astype(F32).astype(BF)
    for b in range(nlat // 256):
        part = dot(pick, leg[b * 256 : (b + 1) * 256, :]).astype(BF)
        for l in range(8):
            perm_leg[l * group + b * 32 : l * group + b * 32 + 32, :] = part[l * 32 : (l + 1) * 32, :]

    across.wait()
    send_inner(partner, 3)

    own1.wait()
    wait_bytes(recv1.at[pl.ds(0, rows - 1)], recv_sem.at[0])
    data = recv1[...].reshape(group, wide)
    hw = perm_leg.shape[1] // 2
    top = float((comps * rows + 2 * hw - 1) * (comps * rows + 2 * hw))
    wave = comp * rows + me
    grids = []
    for h in range(2):
        x = jnp.concatenate(
            [data[:, h * mid + l * cols : h * mid + (l + 1) * cols] for l in range(8)], axis=0
        )
        ph = perm_leg[:, h * hw : (h + 1) * hw]
        spec = dot(x, ph, TN) / nlat
        degree = (2 * iota((1, hw), 1) + wave + h).astype(F32)
        ratio = degree * (degree + 1.0) / top
        factor = 1.0 / (1.0 + kappa[...].T * (ratio * ratio))
        filt = (spec * factor).astype(BF)
        grids.append(dot(ph, filt, NT))
    upper = (grids[0] + grids[1]).astype(BF)
    lower = (grids[0] - grids[1]).astype(BF)
    back = jnp.concatenate(
        [g[l * group : (l + 1) * group, :] for g in (upper, lower) for l in range(8)], axis=1
    )
    send2[...] = back.reshape(rows, 2, wide)

    def send_back(k, _):
        target = lax.rem(me + k, rows)
        pltpu.make_async_remote_copy(
            src_ref=send2.at[target], dst_ref=out_spec.at[me], send_sem=send_sem.at[6], recv_sem=recv_sem.at[6],
            device_id={"row": target}, device_id_type=MESH).start()
        return 0

    lax.fori_loop(1, rows, send_back, 0)
    own2 = pltpu.make_async_copy(send2.at[me], out_spec.at[me], loc_sem.at[3])
    own2.start()

    wait_bytes(gath.at[pl.ds(0, half - 1)], recv_sem.at[2])
    wait_bytes(gath.at[pl.ds(0, half - 1)], recv_sem.at[3])
    total_rows = comps * tile
    held = tile + 8
    sst = gath[:, 0:16, :].reshape(total_rows, cells)
    contribs = gath[:, 16:32, :].reshape(comps * 16, cells)
    src16 = jnp.sum(gath[:, 32:48, :].astype(F32), axis=0).astype(jnp.int32)
    src = jnp.concatenate([src16[0:1, :], src16[1:2, :]], axis=1)
    pos = iota((2 * held, comps * 16), 0)
    pos_f = pos // held
    pos_y = pos - pos_f * held
    pos_y = jnp.where(pos_y < tile + 4, pos_y, pos_y - held)
    pos_y = lax.rem(comp * tile + pos_y + total_rows, total_rows)
    lane = iota((2 * held, comps * 16), 1)
    pick_f = (pos_y == src) & (lax.rem(lane // blocks, 2) == pos_f)
    forcing = dot(jnp.where(pick_f, 1.0, 0.0).astype(BF), contribs)

    to_north.wait()
    to_south.wait()
    wide_slabs = []
    for p in range(count // 2):
        from_south, from_north = nsrecv[0, p], nsrecv[1, p]
        halo_a = jnp.where(row8 < 4, from_south, from_north)
        halo_b = jnp.where(row8 < 4, pltpu.roll(from_south, 4, 0), pltpu.roll(from_north, 4, 0))
        wide_slabs.append(jnp.concatenate([slabs[2 * p], halo_a], axis=0))
        wide_slabs.append(jnp.concatenate([slabs[2 * p + 1], halo_b], axis=0))
    wide_slabs[0] = wide_slabs[0] + forcing[0:held]
    wide_slabs[4] = wide_slabs[4] + forcing[held:]

    lane24 = iota((held, cells), 1)
    westward = jnp.zeros((held, cells), F32)
    eastward = jnp.zeros((held, cells), F32)
    for i, slab in enumerate(wide_slabs):
        own_w = (lane24 >= 4 * i) & (lane24 < 4 * i + 4)
        own_e = (lane24 >= cells - 4 - 4 * i) & (lane24 < cells - 4 * i)
        westward = jnp.where(own_w, pltpu.roll(slab, 4 * i, 1), westward)
        eastward = jnp.where(own_e, pltpu.roll(slab, (cells - 4 * i) % cells, 1), eastward)
    ewpack[0] = westward
    ewpack[1] = eastward
    to_west = pltpu.make_async_remote_copy(
        src_ref=ewpack.at[0], dst_ref=ewrecv.at[0], send_sem=send_sem.at[7], recv_sem=recv_sem.at[7],
        device_id={"row": west}, device_id_type=MESH)
    to_east = pltpu.make_async_remote_copy(
        src_ref=ewpack.at[1], dst_ref=ewrecv.at[1], send_sem=send_sem.at[8], recv_sem=recv_sem.at[8],
        device_id={"row": east}, device_id_type=MESH)
    to_west.start()
    to_east.start()

    heat = jnp.zeros((8, cells), F32)
    prow = iota((8, total_rows), 0)
    plane = iota((8, total_rows), 1)
    hrow = iota((8, cells), 0)
    for k in range(kb):
        want = jnp.full((8, total_rows), -1, jnp.int32)
        for b in range(blocks // kb):
            want = jnp.where(prow == b, srcs[k, b], want)
        picked = dot(jnp.where(plane == want, 1.0, 0.0).astype(BF), sst).astype(BF)
        for b in range(blocks // kb):
            heat = heat + jnp.where(hrow == b, dot(picked, wts[b * kb + k]), 0.0)
    out_heat[...] = heat[0 : blocks // kb, :]

    to_west.wait()
    to_east.wait()
    from_east, from_west = ewrecv[0], ewrecv[1]
    sides = []
    for i in range(count):
        e_part = pltpu.roll(from_east, (cells - 4 * i) % cells, 1)
        w_part = pltpu.roll(from_west, 4 * i, 1)
        sides.append(jnp.where(lane24 < 4, e_part, jnp.where(lane24 >= cells - 4, w_part, 0.0)))
    ypos = iota((held, cells), 0)
    grow = comp * tile + jnp.where(ypos < tile + 4, ypos, ypos - held)
    grow = lax.rem(grow + total_rows, total_rows)
    up_open = (grow != 0).astype(F32)
    down_open = (grow != total_rows - 1).astype(F32)
    first_lane, last_lane = lane24 == 0, lane24 == cells - 1
    state = [(wide_slabs[i], sides[i]) for i in range(8)]
    kh = [(wide_slabs[8 + k], sides[8 + k]) for k in range(4)]
    for _ in range(NSTEP):
        new = []
        for t in range(2):
            for k in range(4):
                core, side = state[t * 4 + k]
                above = state[t * 4 + max(k - 1, 0)]
                below = state[t * 4 + min(k + 1, 3)]
                ce, se = pltpu.roll(core, cells - 1, 1), pltpu.roll(side, cells - 1, 1)
                cw, sw = pltpu.roll(core, 1, 1), pltpu.roll(side, 1, 1)
                easts = (jnp.where(last_lane, se, ce), jnp.where(last_lane, ce, se))
                wests = (jnp.where(first_lane, sw, cw), jnp.where(first_lane, cw, sw))
                pair = []
                for q in range(2):
                    v = state[t * 4 + k][q]
                    up = pltpu.roll(v, 1, 0)
                    down = pltpu.roll(v, held - 1, 0)
                    lateral = (up - v) * up_open + (down - v) * down_open + (easts[q] - v) + (wests[q] - v)
                    vertical = above[q] + below[q] - 2.0 * v
                    pair.append(v + kh[k][q] * lateral + kap_v[k] * vertical)
                new.append(tuple(pair))
        state = new
    for t in range(2):
        for k in range(4):
            out_ocean[t, k] = state[t * 4 + k][0][:tile]

    own2.wait()
    wait_bytes(send2.at[pl.ds(0, rows - 1)], recv_sem.at[6])
    wait_bytes(send1.at[pl.ds(0, rows - 1)], send_sem.at[0])
    wait_bytes(send2.at[pl.ds(0, rows - 1)], send_sem.at[6])
    wait_bytes(gath.at[pl.ds(0, half - 1)], send_sem.at[2])
    wait_bytes(gath.at[pl.ds(0, half - 1)], send_sem.at[3])


def body(
    fourier,
    legendre,
    gauss_weight,
    kappa_spec,
    marine_tracer_fields,
    kappa_h,
    kappa_v,
    air_flux,
    remap_weight,
    remap_source,
):
    rows = lax.axis_size("row")
    comps = lax.axis_size("comp")
    hemis, waves, wide = fourier.shape
    nlat, ns = legendre.shape[1:]
    tracers, levels, tile, cells = marine_tracer_fields.shape
    blocks = remap_weight.shape[0] * remap_weight.shape[2]
    vm = pl.BlockSpec(memory_space=pltpu.VMEM)
    sm = pl.BlockSpec(memory_space=pltpu.SMEM)
    anyspace = pl.BlockSpec(memory_space=pl.ANY)
    spectral, ocean, heat = pl.pallas_call(
        kernel,
        out_shape=(
            jax.ShapeDtypeStruct((waves, 2, wide), BF),
            jax.ShapeDtypeStruct(marine_tracer_fields.shape, F32),
            jax.ShapeDtypeStruct((remap_weight.shape[0], cells), F32),
        ),
        in_specs=[vm, anyspace, sm, vm, vm, vm, sm, vm, anyspace, sm],
        out_specs=(anyspace, vm, vm),
        scratch_shapes=[
            pltpu.VMEM((nlat, ns), BF),
            pltpu.VMEM((blocks, cells, cells), BF),
            pltpu.VMEM((nlat, ns), BF),
            pltpu.VMEM((waves, 2, wide), BF),
            pltpu.VMEM((waves, 2, wide), BF),
            pltpu.VMEM((waves, 2, wide), BF),
            pltpu.VMEM((comps, 48, cells), BF),
            pltpu.VMEM((2, 6, 8, cells), F32),
            pltpu.VMEM((2, 6, 8, cells), F32),
            pltpu.VMEM((2, tile + 8, cells), F32),
            pltpu.VMEM((2, tile + 8, cells), F32),
            pltpu.SemaphoreType.DMA((4,)),
            pltpu.SemaphoreType.DMA((9,)),
            pltpu.SemaphoreType.DMA((9,)),
        ],
        compiler_params=pltpu.CompilerParams(
            collective_id=0, has_side_effects=True, vmem_limit_bytes=48 * 2**20
        ),
    )(
        fourier,
        legendre[0],
        gauss_weight,
        kappa_spec.astype(F32).reshape(1, -1),
        marine_tracer_fields,
        kappa_h,
        kappa_v,
        air_flux,
        remap_weight.reshape(blocks, cells, cells),
        remap_source[:, 0, :].T,
    )
    spectral = spectral.reshape(waves, 2, hemis, wide // 2)
    spectral = jnp.transpose(spectral, (2, 0, 1, 3)).reshape(fourier.shape)
    return spectral, ocean, heat


def solution(mesh):
    return jax.shard_map(
        body,
        mesh=mesh,
        in_specs=(
            P(None, "comp", "row"),
            P(("comp", "row"), None, None),
            P(),
            P(),
            P(None, None, "comp", "row"),
            P(None, "comp", "row"),
            P(),
            P(None, "comp", "row"),
            P("comp", "row", None, None, None),
            P("comp", "row", None),
        ),
        out_specs=(P(None, "comp", "row"), P(None, None, "comp", "row"), P("comp", "row")),
        check_vma=False,
    )
```

```python
import functools

import jax
import jax.numpy as jnp
from jax import lax
from jax.experimental import pallas as pl
from jax.experimental.pallas import tpu as pltpu
from jax.sharding import PartitionSpec as P

NSTEP = 4
MESH = pl.DeviceIdType.MESH
BF = jnp.bfloat16
F32 = jnp.float32
NN = (((1,), (0,)), ((), ()))
NT = (((1,), (1,)), ((), ()))
TN = (((0,), (0,)), ((), ()))


def dot(a, b, dims=NN):
    return lax.dot_general(a, b, dims, preferred_element_type=F32)


def iota(shape, axis):
    return lax.broadcasted_iota(jnp.int32, shape, axis)


def wait_bytes(ref, sem):
    pltpu.make_async_copy(ref, ref, sem).wait()


def kernel(
    four_hbm, leg_hbm, gauss_hbm, kappa_hbm, fields_hbm, kap_h_hbm, kap_v_hbm, flux_hbm, wts_hbm, srcs_hbm,
    out_spec, out_ocean, out_heat,
    four, leg, gauss, kappa, fields, kap_h, kap_v, flux, wts, srcs,
    perm_leg, send1, recv1, send2, gath, nspack, nsrecv, ewpack, ewrecv,
    loc_sem, send_sem, recv_sem, ready, upper,
):
    rows = lax.axis_size("row")
    comps = lax.axis_size("comp")
    me = lax.axis_index("row")
    comp = lax.axis_index("comp")
    half = comps // 2
    zhi = comp // half
    inner = lax.rem(comp, half)
    partner = lax.rem(comp + half, comps)
    north = lax.rem(comp + comps - 1, comps)
    south = lax.rem(comp + 1, comps)
    west = lax.rem(me + rows - 1, rows)
    east = lax.rem(me + 1, rows)

    pairs = (
        (four_hbm, four), (gauss_hbm, gauss), (flux_hbm, flux), (srcs_hbm, srcs), (fields_hbm, fields), (wts_hbm, wts),
        (kap_h_hbm, kap_h), (kap_v_hbm, kap_v), (kappa_hbm, kappa), (leg_hbm, leg),
    )
    loads = [pltpu.make_async_copy(a, b, loc_sem.at[2 + i]) for i, (a, b) in enumerate(pairs)]
    for load in loads:
        load.start()

    ahead = 1 - 2 * zhi
    earlier = jnp.where(zhi == 0, me, rows - 1 - me)
    later = rows - 1 - earlier
    at_end = jnp.where((inner == 0) | (inner == half - 1), 1, 0)
    across_end = jnp.where(inner == 0, north, south)
    barrier = pltpu.get_barrier_semaphore()

    def greet_row(k, _):
        pl.semaphore_signal(barrier, inc=1, device_id={"row": me + ahead * k}, device_id_type=MESH)
        return 0

    def greet_comp(k, _):
        target = zhi * half + lax.rem(inner + k, half)
        pl.semaphore_signal(barrier, inc=1, device_id={"comp": target}, device_id_type=MESH)
        return 0

    lax.fori_loop(1, later + 1, greet_row, 0)
    lax.fori_loop(1, half, greet_comp, 0)

    @pl.when(zhi == 0)
    def _():
        pl.semaphore_signal(barrier, inc=1, device_id={"comp": partner}, device_id_type=MESH)

    @pl.when((zhi == 0) & (at_end == 1))
    def _():
        pl.semaphore_signal(barrier, inc=1, device_id={"comp": across_end}, device_id_type=MESH)

    wide = four.shape[2]
    cols = kappa.shape[0]
    lats = wide // cols
    mid = wide // 2
    lane_lat = iota((1, wide), 1) // cols
    loads[0].wait()
    loads[1].wait()
    weight = jnp.zeros((1, wide), F32)
    for l in range(lats):
        weight = jnp.where(lane_lat == l, gauss[me * lats + l], weight)
    n = four[0].astype(F32)
    s = four[1].astype(F32)
    even = (weight * (n + s)).astype(BF)
    odd = (weight * (n - s)).astype(BF)
    first = jnp.concatenate([even[:, :mid], odd[:, :mid]], axis=1)
    second = jnp.concatenate([even[:, mid:], odd[:, mid:]], axis=1)
    send1[:, 0, :] = first
    send1[:, 1, :] = second

    pl.semaphore_wait(barrier, earlier + half - 1 + zhi * (1 + at_end))

    def answer_row(k, _):
        pl.semaphore_signal(ready.at[me], inc=1, device_id={"row": me - ahead * k}, device_id_type=MESH)
        return 0

    lax.fori_loop(1, earlier + 1, answer_row, 0)

    @pl.when(zhi == 1)
    def _():
        pl.semaphore_signal(upper, inc=1, device_id={"comp": partner}, device_id_type=MESH)

    @pl.when((zhi == 1) & (at_end == 1))
    def _():
        pl.semaphore_signal(upper, inc=1, device_id={"comp": across_end}, device_id_type=MESH)

    def forward_to(target):
        pltpu.make_async_remote_copy(
            src_ref=send1.at[target], dst_ref=recv1.at[me], send_sem=send_sem.at[0], recv_sem=recv_sem.at[0],
            device_id={"row": target}, device_id_type=MESH).start()

    def forward_earlier(k, _):
        forward_to(me - ahead * (earlier + 1 - k))
        return 0

    lax.fori_loop(1, earlier + 1, forward_earlier, 0)
    own1 = pltpu.make_async_copy(send1.at[me], recv1.at[me], loc_sem.at[0])
    own1.start()

    for load in loads[2:6]:
        load.wait()
    tile = fields.shape[2]
    cells = fields.shape[3]
    blocks = wts.shape[0]
    kb = srcs.shape[0]
    row16 = iota((16, cells), 0)
    lane16 = iota((16, cells), 1)
    rep = jnp.zeros((16, cells), F32)
    for f in range(2):
        for j in range(blocks):
            rep = jnp.where(row16 == f * blocks + j, flux[f, j // kb, :].astype(F32)[None, :], rep)
    contrib = jnp.zeros((16, cells), F32)
    for j in range(blocks):
        only = jnp.where(lax.rem(row16, blocks) == j, rep, 0.0).astype(BF)
        contrib = contrib + dot(only, wts[j], NT)
    src_row = jnp.zeros((16, cells), F32)
    for j in range(blocks):
        hit = (lane16 // 16 == inner) & (lax.rem(lane16, blocks) == j) & (row16 == zhi)
        src_row = jnp.where(hit, srcs[j % kb, j // kb].astype(F32), src_row)
    gath[comp, 0:16, :] = fields[0, 0].astype(BF)
    gath[comp, 16:32, :] = contrib.astype(BF)
    gath[comp, 32:48, :] = src_row.astype(BF)
    across = pltpu.make_async_remote_copy(
        src_ref=gath.at[comp], dst_ref=gath.at[comp], send_sem=send_sem.at[1], recv_sem=recv_sem.at[1],
        device_id={"comp": partner}, device_id_type=MESH)

    @pl.when(zhi == 1)
    def _():
        across.start()

    def send_inner(slot, which):
        def step(k, _):
            target = zhi * half + lax.rem(inner + k, half)
            pltpu.make_async_remote_copy(
                src_ref=gath.at[slot], dst_ref=gath.at[slot], send_sem=send_sem.at[which], recv_sem=recv_sem.at[which],
                device_id={"comp": target}, device_id_type=MESH).start()
            return 0

        lax.fori_loop(1, half, step, 0)

    send_inner(comp, 2)

    loads[6].wait()
    slabs = [fields[t, k] for t in range(2) for k in range(4)] + [kap_h[k] for k in range(4)]
    count = len(slabs)
    row8 = iota((8, cells), 0)
    for p in range(count // 2):
        a, b = slabs[2 * p], slabs[2 * p + 1]
        nspack[0, p] = jnp.where(row8 < 4, a[:8], pltpu.roll(b[:8], 4, 0))
        nspack[1, p] = jnp.where(row8 >= 4, a[tile - 8 :], pltpu.roll(b[tile - 8 :], 4, 0))
    to_north = pltpu.make_async_remote_copy(
        src_ref=nspack.at[0], dst_ref=nsrecv.at[0], send_sem=send_sem.at[4], recv_sem=recv_sem.at[4],
        device_id={"comp": north}, device_id_type=MESH)
    to_south = pltpu.make_async_remote_copy(
        src_ref=nspack.at[1], dst_ref=nsrecv.at[1], send_sem=send_sem.at[5], recv_sem=recv_sem.at[5],
        device_id={"comp": south}, device_id_type=MESH)
    north_first = (zhi == 1) | (inner > 0)
    south_first = (zhi == 1) | (inner < half - 1)

    @pl.when(north_first)
    def _():
        to_north.start()

    @pl.when(south_first)
    def _():
        to_south.start()

    for load in loads[7:]:
        load.wait()
    nlat = leg.shape[0]
    group = 2 * rows
    gi = iota((256, 256), 0)
    pick = (iota((256, 256), 1) == 8 * lax.rem(gi, 32) + gi // 32).astype(F32).astype(BF)
    for b in range(nlat // 256):
        part = dot(pick, leg[b * 256 : (b + 1) * 256, :]).astype(BF)
        for l in range(8):
            perm_leg[l * group + b * 32 : l * group + b * 32 + 32, :] = part[l * 32 : (l + 1) * 32, :]

    def forward_later(k, _):
        target = me + ahead * k
        pl.semaphore_wait(ready.at[target], 1)
        forward_to(target)
        return 0

    lax.fori_loop(1, later + 1, forward_later, 0)

    own1.wait()
    wait_bytes(recv1.at[pl.ds(0, rows - 1)], recv_sem.at[0])
    data = recv1[...].reshape(group, wide)
    hw = perm_leg.shape[1] // 2
    top = float((comps * rows + 2 * hw - 1) * (comps * rows + 2 * hw))
    wave = comp * rows + me
    kappa_col = kappa[...].astype(F32).reshape(1, cols).T
    grids = []
    for h in range(2):
        x = jnp.concatenate(
            [data[:, h * mid + l * cols : h * mid + (l + 1) * cols] for l in range(8)], axis=0
        )
        ph = perm_leg[:, h * hw : (h + 1) * hw]
        spec = dot(x, ph, TN) / nlat
        degree = (2 * iota((1, hw), 1) + wave + h).astype(F32)
        ratio = degree * (degree + 1.0) / top
        factor = 1.0 / (1.0 + kappa_col * (ratio * ratio))
        filt = (spec * factor).astype(BF)
        grids.append(dot(ph, filt, NT))
    north_grid = (grids[0] + grids[1]).astype(BF)
    south_grid = (grids[0] - grids[1]).astype(BF)
    back = jnp.concatenate(
        [g[l * group : (l + 1) * group, :] for g in (north_grid, south_grid) for l in range(8)], axis=1
    )
    send2[...] = back.reshape(rows, 2, wide)

    def send_back(k, _):
        step = (k + 1) // 2
        turn = jnp.where(lax.rem(k, 2) == 1, step, rows - step)
        target = lax.rem(me + turn, rows)
        pltpu.make_async_remote_copy(
            src_ref=send2.at[target], dst_ref=out_spec.at[me], send_sem=send_sem.at[6], recv_sem=recv_sem.at[6],
            device_id={"row": target}, device_id_type=MESH).start()
        return 0

    lax.fori_loop(1, rows, send_back, 0)
    own2 = pltpu.make_async_copy(send2.at[me], out_spec.at[me], loc_sem.at[1])
    own2.start()

    @pl.when(zhi == 0)
    def _():
        pl.semaphore_wait(upper, 1 + at_end)
        across.start()

    @pl.when(jnp.logical_not(north_first))
    def _():
        to_north.start()

    @pl.when(jnp.logical_not(south_first))
    def _():
        to_south.start()

    across.wait_recv()
    send_inner(partner, 3)

    wait_bytes(gath.at[pl.ds(0, half - 1)], recv_sem.at[2])
    wait_bytes(gath.at[pl.ds(0, half - 1)], recv_sem.at[3])
    total_rows = comps * tile
    held = tile + 8
    sst = gath[:, 0:16, :].reshape(total_rows, cells)
    contribs = gath[:, 16:32, :].reshape(comps * 16, cells)
    src16 = jnp.sum(gath[:, 32:48, :].astype(F32), axis=0).astype(jnp.int32)
    src = jnp.concatenate([src16[0:1, :], src16[1:2, :]], axis=1)
    pos = iota((2 * held, comps * 16), 0)
    pos_f = pos // held
    pos_y = pos - pos_f * held
    pos_y = jnp.where(pos_y < tile + 4, pos_y, pos_y - held)
    pos_y = lax.rem(comp * tile + pos_y + total_rows, total_rows)
    lane = iota((2 * held, comps * 16), 1)
    pick_f = (pos_y == src) & (lax.rem(lane // blocks, 2) == pos_f)
    forcing = dot(jnp.where(pick_f, 1.0, 0.0).astype(BF), contribs)

    to_north.wait()
    to_south.wait()
    wide_slabs = []
    for p in range(count // 2):
        from_south, from_north = nsrecv[0, p], nsrecv[1, p]
        halo_a = jnp.where(row8 < 4, from_south, from_north)
        halo_b = jnp.where(row8 < 4, pltpu.roll(from_south, 4, 0), pltpu.roll(from_north, 4, 0))
        wide_slabs.append(jnp.concatenate([slabs[2 * p], halo_a], axis=0))
        wide_slabs.append(jnp.concatenate([slabs[2 * p + 1], halo_b], axis=0))
    wide_slabs[0] = wide_slabs[0] + forcing[0:held]
    wide_slabs[4] = wide_slabs[4] + forcing[held:]

    lane24 = iota((held, cells), 1)
    westward = jnp.zeros((held, cells), F32)
    eastward = jnp.zeros((held, cells), F32)
    for i, slab in enumerate(wide_slabs):
        own_w = (lane24 >= 4 * i) & (lane24 < 4 * i + 4)
        own_e = (lane24 >= cells - 4 - 4 * i) & (lane24 < cells - 4 * i)
        westward = jnp.where(own_w, pltpu.roll(slab, 4 * i, 1), westward)
        eastward = jnp.where(own_e, pltpu.roll(slab, (cells - 4 * i) % cells, 1), eastward)
    ewpack[0] = westward
    ewpack[1] = eastward
    to_west = pltpu.make_async_remote_copy(
        src_ref=ewpack.at[0], dst_ref=ewrecv.at[0], send_sem=send_sem.at[7], recv_sem=recv_sem.at[7],
        device_id={"row": west}, device_id_type=MESH)
    to_east = pltpu.make_async_remote_copy(
        src_ref=ewpack.at[1], dst_ref=ewrecv.at[1], send_sem=send_sem.at[8], recv_sem=recv_sem.at[8],
        device_id={"row": east}, device_id_type=MESH)
    to_west.start()
    to_east.start()

    heat = jnp.zeros((8, cells), F32)
    prow = iota((8, total_rows), 0)
    plane = iota((8, total_rows), 1)
    hrow = iota((8, cells), 0)
    for k in range(kb):
        want = jnp.full((8, total_rows), -1, jnp.int32)
        for b in range(blocks // kb):
            want = jnp.where(prow == b, srcs[k, b], want)
        picked = dot(jnp.where(plane == want, 1.0, 0.0).astype(BF), sst).astype(BF)
        for b in range(blocks // kb):
            heat = heat + jnp.where(hrow == b, dot(picked, wts[b * kb + k]), 0.0)
    out_heat[...] = heat[0 : blocks // kb, :]

    to_west.wait()
    to_east.wait()
    from_east, from_west = ewrecv[0], ewrecv[1]
    sides = []
    for i in range(count):
        e_part = pltpu.roll(from_east, (cells - 4 * i) % cells, 1)
        w_part = pltpu.roll(from_west, 4 * i, 1)
        sides.append(jnp.where(lane24 < 4, e_part, jnp.where(lane24 >= cells - 4, w_part, 0.0)))
    ypos = iota((held, cells), 0)
    grow = comp * tile + jnp.where(ypos < tile + 4, ypos, ypos - held)
    grow = lax.rem(grow + total_rows, total_rows)
    up_open = (grow != 0).astype(F32)
    down_open = (grow != total_rows - 1).astype(F32)
    first_lane, last_lane = lane24 == 0, lane24 == cells - 1
    state = [(wide_slabs[i], sides[i]) for i in range(8)]
    kh = [(wide_slabs[8 + k], sides[8 + k]) for k in range(4)]
    for _ in range(NSTEP):
        new = []
        for t in range(2):
            for k in range(4):
                core, side = state[t * 4 + k]
                above = state[t * 4 + max(k - 1, 0)]
                below = state[t * 4 + min(k + 1, 3)]
                ce, se = pltpu.roll(core, cells - 1, 1), pltpu.roll(side, cells - 1, 1)
                cw, sw = pltpu.roll(core, 1, 1), pltpu.roll(side, 1, 1)
                easts = (jnp.where(last_lane, se, ce), jnp.where(last_lane, ce, se))
                wests = (jnp.where(first_lane, sw, cw), jnp.where(first_lane, cw, sw))
                pair = []
                for q in range(2):
                    v = state[t * 4 + k][q]
                    up = pltpu.roll(v, 1, 0)
                    down = pltpu.roll(v, held - 1, 0)
                    lateral = (up - v) * up_open + (down - v) * down_open + (easts[q] - v) + (wests[q] - v)
                    vertical = above[q] + below[q] - 2.0 * v
                    pair.append(v + kh[k][q] * lateral + kap_v[k] * vertical)
                new.append(tuple(pair))
        state = new
    for t in range(2):
        for k in range(4):
            out_ocean[t, k] = state[t * 4 + k][0][:tile]

    own2.wait()
    across.wait_send()
    wait_bytes(send2.at[pl.ds(0, rows - 1)], recv_sem.at[6])
    wait_bytes(send1.at[pl.ds(0, rows - 1)], send_sem.at[0])
    wait_bytes(send2.at[pl.ds(0, rows - 1)], send_sem.at[6])
    wait_bytes(gath.at[pl.ds(0, half - 1)], send_sem.at[2])
    wait_bytes(gath.at[pl.ds(0, half - 1)], send_sem.at[3])


def body(
    fourier,
    legendre,
    gauss_weight,
    kappa_spec,
    marine_tracer_fields,
    kappa_h,
    kappa_v,
    air_flux,
    remap_weight,
    remap_source,
):
    rows = lax.axis_size("row")
    comps = lax.axis_size("comp")
    hemis, waves, wide = fourier.shape
    nlat, ns = legendre.shape[1:]
    tracers, levels, tile, cells = marine_tracer_fields.shape
    blocks = remap_weight.shape[0] * remap_weight.shape[2]
    vm = pl.BlockSpec(memory_space=pltpu.VMEM)
    anyspace = pl.BlockSpec(memory_space=pl.ANY)
    spectral, ocean, heat = pl.pallas_call(
        kernel,
        out_shape=(
            jax.ShapeDtypeStruct((waves, 2, wide), BF),
            jax.ShapeDtypeStruct(marine_tracer_fields.shape, F32),
            jax.ShapeDtypeStruct((remap_weight.shape[0], cells), F32),
        ),
        in_specs=[anyspace] * 10,
        out_specs=(anyspace, vm, vm),
        scratch_shapes=[
            pltpu.VMEM(fourier.shape, BF),
            pltpu.VMEM((nlat, ns), BF),
            pltpu.SMEM(gauss_weight.shape, F32),
            pltpu.VMEM(kappa_spec.shape, BF),
            pltpu.VMEM(marine_tracer_fields.shape, F32),
            pltpu.VMEM(kappa_h.shape, F32),
            pltpu.SMEM(kappa_v.shape, F32),
            pltpu.VMEM(air_flux.shape, BF),
            pltpu.VMEM((blocks, cells, cells), BF),
            pltpu.SMEM(remap_source.shape[:1:-1] + remap_source.shape[:1], jnp.int32),
            pltpu.VMEM((nlat, ns), BF),
            pltpu.VMEM((waves, 2, wide), BF),
            pltpu.VMEM((waves, 2, wide), BF),
            pltpu.VMEM((waves, 2, wide), BF),
            pltpu.VMEM((comps, 48, cells), BF),
            pltpu.VMEM((2, 6, 8, cells), F32),
            pltpu.VMEM((2, 6, 8, cells), F32),
            pltpu.VMEM((2, tile + 8, cells), F32),
            pltpu.VMEM((2, tile + 8, cells), F32),
            pltpu.SemaphoreType.DMA((12,)),
            pltpu.SemaphoreType.DMA((9,)),
            pltpu.SemaphoreType.DMA((9,)),
            pltpu.SemaphoreType.REGULAR((rows,)),
            pltpu.SemaphoreType.REGULAR,
        ],
        compiler_params=pltpu.CompilerParams(
            collective_id=0, has_side_effects=True, vmem_limit_bytes=60 * 2**20
        ),
    )(
        fourier,
        legendre[0],
        gauss_weight,
        kappa_spec,
        marine_tracer_fields,
        kappa_h,
        kappa_v,
        air_flux,
        remap_weight.reshape(blocks, cells, cells),
        remap_source[:, 0, :].T,
    )
    spectral = spectral.reshape(waves, 2, hemis, wide // 2)
    spectral = jnp.transpose(spectral, (2, 0, 1, 3)).reshape(fourier.shape)
    return spectral, ocean, heat


def solution(mesh):
    return jax.shard_map(
        body,
        mesh=mesh,
        in_specs=(
            P(None, "comp", "row"),
            P(("comp", "row"), None, None),
            P(),
            P(),
            P(None, None, "comp", "row"),
            P(None, "comp", "row"),
            P(),
            P(None, "comp", "row"),
            P("comp", "row", None, None, None),
            P("comp", "row", None),
        ),
        out_specs=(P(None, "comp", "row"), P(None, None, "comp", "row"), P("comp", "row")),
        check_vma=False,
    )
```

```python
import functools

import jax
import jax.numpy as jnp
from jax import lax
from jax.experimental import pallas as pl
from jax.experimental.pallas import tpu as pltpu
from jax.sharding import PartitionSpec as P

NSTEP = 4
MESH = pl.DeviceIdType.MESH
BF = jnp.bfloat16
F32 = jnp.float32
NN = (((1,), (0,)), ((), ()))
NT = (((1,), (1,)), ((), ()))
TN = (((0,), (0,)), ((), ()))


def dot(a, b, dims=NN):
    return lax.dot_general(a, b, dims, preferred_element_type=F32)


def iota(shape, axis):
    return lax.broadcasted_iota(jnp.int32, shape, axis)


def wait_bytes(ref, sem):
    pltpu.make_async_copy(ref, ref, sem).wait()


def kernel(
    four_hbm, leg_hbm, gauss_hbm, kappa_hbm, fields_hbm, kap_h_hbm, kap_v_hbm, flux_hbm, wts_hbm, srcs_hbm,
    out_spec, out_ocean, out_heat,
    four, leg, gauss, kappa, fields, kap_h, kap_v, flux, wts, srcs,
    perm_leg, send1, recv1, send2, gath, nspack, nsrecv, ewpack, ewrecv,
    loc_sem, send_sem, recv_sem, ready, upper,
):
    rows = lax.axis_size("row")
    comps = lax.axis_size("comp")
    me = lax.axis_index("row")
    comp = lax.axis_index("comp")
    half = comps // 2
    zhi = comp // half
    inner = lax.rem(comp, half)
    partner = lax.rem(comp + half, comps)
    north = lax.rem(comp + comps - 1, comps)
    south = lax.rem(comp + 1, comps)
    west = lax.rem(me + rows - 1, rows)
    east = lax.rem(me + 1, rows)

    pairs = (
        (four_hbm, four), (gauss_hbm, gauss), (flux_hbm, flux), (srcs_hbm, srcs), (fields_hbm, fields), (wts_hbm, wts),
        (kap_h_hbm, kap_h), (kap_v_hbm, kap_v), (kappa_hbm, kappa), (leg_hbm, leg),
    )
    loads = [pltpu.make_async_copy(a, b, loc_sem.at[2 + i]) for i, (a, b) in enumerate(pairs)]
    for load in loads:
        load.start()

    ahead = 1 - 2 * zhi
    earlier = jnp.where(zhi == 0, me, rows - 1 - me)
    later = rows - 1 - earlier
    at_end = jnp.where((inner == 0) | (inner == half - 1), 1, 0)
    across_end = jnp.where(inner == 0, north, south)
    barrier = pltpu.get_barrier_semaphore()

    def greet_row(k, _):
        pl.semaphore_signal(barrier, inc=1, device_id={"row": me + ahead * k}, device_id_type=MESH)
        return 0

    def greet_comp(k, _):
        target = zhi * half + lax.rem(inner + k, half)
        pl.semaphore_signal(barrier, inc=1, device_id={"comp": target}, device_id_type=MESH)
        return 0

    lax.fori_loop(1, later + 1, greet_row, 0)
    lax.fori_loop(1, half, greet_comp, 0)

    @pl.when(zhi == 0)
    def _():
        pl.semaphore_signal(barrier, inc=1, device_id={"comp": partner}, device_id_type=MESH)

    @pl.when((zhi == 0) & (at_end == 1))
    def _():
        pl.semaphore_signal(barrier, inc=1, device_id={"comp": across_end}, device_id_type=MESH)

    wide = four.shape[2]
    cols = kappa.shape[0]
    lats = wide // cols
    mid = wide // 2
    lane_lat = iota((1, wide), 1) // cols
    loads[0].wait()
    loads[1].wait()
    weight = jnp.zeros((1, wide), F32)
    for l in range(lats):
        weight = jnp.where(lane_lat == l, gauss[me * lats + l], weight)
    n = four[0].astype(F32)
    s = four[1].astype(F32)
    even = (weight * (n + s)).astype(BF)
    odd = (weight * (n - s)).astype(BF)
    first = jnp.concatenate([even[:, :mid], odd[:, :mid]], axis=1)
    second = jnp.concatenate([even[:, mid:], odd[:, mid:]], axis=1)
    send1[:, 0, :] = first
    send1[:, 1, :] = second

    pl.semaphore_wait(barrier, earlier + half - 1 + zhi * (1 + at_end))

    def answer_row(k, _):
        pl.semaphore_signal(ready.at[me], inc=1, device_id={"row": me - ahead * k}, device_id_type=MESH)
        return 0

    lax.fori_loop(1, earlier + 1, answer_row, 0)

    @pl.when(zhi == 1)
    def _():
        pl.semaphore_signal(upper, inc=1, device_id={"comp": partner}, device_id_type=MESH)

    @pl.when((zhi == 1) & (at_end == 1))
    def _():
        pl.semaphore_signal(upper, inc=1, device_id={"comp": across_end}, device_id_type=MESH)

    def forward_to(target):
        pltpu.make_async_remote_copy(
            src_ref=send1.at[target], dst_ref=recv1.at[me], send_sem=send_sem.at[0], recv_sem=recv_sem.at[0],
            device_id={"row": target}, device_id_type=MESH).start()

    def forward_earlier(k, _):
        forward_to(me - ahead * (earlier + 1 - k))
        return 0

    lax.fori_loop(1, earlier + 1, forward_earlier, 0)
    own1 = pltpu.make_async_copy(send1.at[me], recv1.at[me], loc_sem.at[0])
    own1.start()

    for load in loads[2:6]:
        load.wait()
    tile = fields.shape[2]
    cells = fields.shape[3]
    blocks = wts.shape[0]
    kb = srcs.shape[0]
    row16 = iota((16, cells), 0)
    lane16 = iota((16, cells), 1)
    rep = jnp.zeros((16, cells), F32)
    for f in range(2):
        for j in range(blocks):
            rep = jnp.where(row16 == f * blocks + j, flux[f, j // kb, :].astype(F32)[None, :], rep)
    contrib = jnp.zeros((16, cells), F32)
    for j in range(blocks):
        only = jnp.where(lax.rem(row16, blocks) == j, rep, 0.0).astype(BF)
        contrib = contrib + dot(only, wts[j], NT)
    src_row = jnp.zeros((16, cells), F32)
    for j in range(blocks):
        hit = (lane16 // 16 == inner) & (lax.rem(lane16, blocks) == j) & (row16 == zhi)
        src_row = jnp.where(hit, srcs[j % kb, j // kb].astype(F32), src_row)
    gath[comp, 0:16, :] = fields[0, 0].astype(BF)
    gath[comp, 16:32, :] = contrib.astype(BF)
    gath[comp, 32:48, :] = src_row.astype(BF)
    across = pltpu.make_async_remote_copy(
        src_ref=gath.at[comp], dst_ref=gath.at[comp], send_sem=send_sem.at[1], recv_sem=recv_sem.at[1],
        device_id={"comp": partner}, device_id_type=MESH)

    @pl.when(zhi == 1)
    def _():
        across.start()

    def send_inner(slot, which):
        def step(k, _):
            target = zhi * half + lax.rem(inner + k, half)
            pltpu.make_async_remote_copy(
                src_ref=gath.at[slot], dst_ref=gath.at[slot], send_sem=send_sem.at[which], recv_sem=recv_sem.at[which],
                device_id={"comp": target}, device_id_type=MESH).start()
            return 0

        lax.fori_loop(1, half, step, 0)

    send_inner(comp, 2)

    loads[6].wait()
    slabs = [fields[t, k] for t in range(2) for k in range(4)] + [kap_h[k] for k in range(4)]
    count = len(slabs)
    row8 = iota((8, cells), 0)
    for p in range(count // 2):
        a, b = slabs[2 * p], slabs[2 * p + 1]
        nspack[0, p] = jnp.where(row8 < 4, a[:8], pltpu.roll(b[:8], 4, 0))
        nspack[1, p] = jnp.where(row8 >= 4, a[tile - 8 :], pltpu.roll(b[tile - 8 :], 4, 0))
    to_north = pltpu.make_async_remote_copy(
        src_ref=nspack.at[0], dst_ref=nsrecv.at[0], send_sem=send_sem.at[4], recv_sem=recv_sem.at[4],
        device_id={"comp": north}, device_id_type=MESH)
    to_south = pltpu.make_async_remote_copy(
        src_ref=nspack.at[1], dst_ref=nsrecv.at[1], send_sem=send_sem.at[5], recv_sem=recv_sem.at[5],
        device_id={"comp": south}, device_id_type=MESH)
    north_first = (zhi == 1) | (inner > 0)
    south_first = (zhi == 1) | (inner < half - 1)

    @pl.when(north_first)
    def _():
        to_north.start()

    @pl.when(south_first)
    def _():
        to_south.start()

    for load in loads[7:]:
        load.wait()
    nlat = leg.shape[0]
    group = 2 * rows
    gi = iota((256, 256), 0)
    pick = (iota((256, 256), 1) == 8 * lax.rem(gi, 32) + gi // 32).astype(F32).astype(BF)
    for b in range(nlat // 256):
        part = dot(pick, leg[b * 256 : (b + 1) * 256, :]).astype(BF)
        for l in range(8):
            perm_leg[l * group + b * 32 : l * group + b * 32 + 32, :] = part[l * 32 : (l + 1) * 32, :]

    def forward_later(k, _):
        target = me + ahead * k
        pl.semaphore_wait(ready.at[target], 1)
        forward_to(target)
        return 0

    lax.fori_loop(1, later + 1, forward_later, 0)

    own1.wait()
    wait_bytes(recv1.at[pl.ds(0, rows - 1)], recv_sem.at[0])
    data = recv1[...].reshape(group, wide)
    hw = perm_leg.shape[1] // 2
    top = float((comps * rows + 2 * hw - 1) * (comps * rows + 2 * hw))
    wave = comp * rows + me
    kappa_col = kappa[...].astype(F32).reshape(1, cols).T
    grids = []
    for h in range(2):
        x = jnp.concatenate(
            [data[:, h * mid + l * cols : h * mid + (l + 1) * cols] for l in range(8)], axis=0
        )
        ph = perm_leg[:, h * hw : (h + 1) * hw]
        spec = dot(x, ph, TN) / nlat
        degree = (2 * iota((1, hw), 1) + wave + h).astype(F32)
        ratio = degree * (degree + 1.0) / top
        factor = 1.0 / (1.0 + kappa_col * (ratio * ratio))
        filt = (spec * factor).astype(BF)
        grids.append(dot(ph, filt, NT))
    north_grid = (grids[0] + grids[1]).astype(BF)
    south_grid = (grids[0] - grids[1]).astype(BF)
    back = jnp.concatenate(
        [g[l * group : (l + 1) * group, :] for g in (north_grid, south_grid) for l in range(8)], axis=1
    )
    send2[...] = back.reshape(rows, 2, wide)

    @pl.when(zhi == 0)
    def _():
        pl.semaphore_wait(upper, 1 + at_end)
        across.start()

    @pl.when(jnp.logical_not(north_first))
    def _():
        to_north.start()

    @pl.when(jnp.logical_not(south_first))
    def _():
        to_south.start()

    across.wait_recv()
    send_inner(partner, 3)

    def send_back(k, _):
        step = (k + 1) // 2
        turn = jnp.where(lax.rem(k, 2) == 1, step, rows - step)
        target = lax.rem(me + turn, rows)
        pltpu.make_async_remote_copy(
            src_ref=send2.at[target], dst_ref=out_spec.at[me], send_sem=send_sem.at[6], recv_sem=recv_sem.at[6],
            device_id={"row": target}, device_id_type=MESH).start()
        return 0

    lax.fori_loop(1, rows // 2 + 1, send_back, 0)
    own2 = pltpu.make_async_copy(send2.at[me], out_spec.at[me], loc_sem.at[1])
    own2.start()

    wait_bytes(gath.at[pl.ds(0, half - 1)], recv_sem.at[2])
    wait_bytes(gath.at[pl.ds(0, half - 1)], recv_sem.at[3])
    total_rows = comps * tile
    held = tile + 8
    sst = gath[:, 0:16, :].reshape(total_rows, cells)
    contribs = gath[:, 16:32, :].reshape(comps * 16, cells)
    src16 = jnp.sum(gath[:, 32:48, :].astype(F32), axis=0).astype(jnp.int32)
    src = jnp.concatenate([src16[0:1, :], src16[1:2, :]], axis=1)
    pos = iota((2 * held, comps * 16), 0)
    pos_f = pos // held
    pos_y = pos - pos_f * held
    pos_y = jnp.where(pos_y < tile + 4, pos_y, pos_y - held)
    pos_y = lax.rem(comp * tile + pos_y + total_rows, total_rows)
    lane = iota((2 * held, comps * 16), 1)
    pick_f = (pos_y == src) & (lax.rem(lane // blocks, 2) == pos_f)
    forcing = dot(jnp.where(pick_f, 1.0, 0.0).astype(BF), contribs)

    to_north.wait()
    to_south.wait()
    wide_slabs = []
    for p in range(count // 2):
        from_south, from_north = nsrecv[0, p], nsrecv[1, p]
        halo_a = jnp.where(row8 < 4, from_south, from_north)
        halo_b = jnp.where(row8 < 4, pltpu.roll(from_south, 4, 0), pltpu.roll(from_north, 4, 0))
        wide_slabs.append(jnp.concatenate([slabs[2 * p], halo_a], axis=0))
        wide_slabs.append(jnp.concatenate([slabs[2 * p + 1], halo_b], axis=0))
    wide_slabs[0] = wide_slabs[0] + forcing[0:held]
    wide_slabs[4] = wide_slabs[4] + forcing[held:]

    lane24 = iota((held, cells), 1)
    westward = jnp.zeros((held, cells), F32)
    eastward = jnp.zeros((held, cells), F32)
    for i, slab in enumerate(wide_slabs):
        own_w = (lane24 >= 4 * i) & (lane24 < 4 * i + 4)
        own_e = (lane24 >= cells - 4 - 4 * i) & (lane24 < cells - 4 * i)
        westward = jnp.where(own_w, pltpu.roll(slab, 4 * i, 1), westward)
        eastward = jnp.where(own_e, pltpu.roll(slab, (cells - 4 * i) % cells, 1), eastward)
    ewpack[0] = westward
    ewpack[1] = eastward
    to_west = pltpu.make_async_remote_copy(
        src_ref=ewpack.at[0], dst_ref=ewrecv.at[0], send_sem=send_sem.at[7], recv_sem=recv_sem.at[7],
        device_id={"row": west}, device_id_type=MESH)
    to_east = pltpu.make_async_remote_copy(
        src_ref=ewpack.at[1], dst_ref=ewrecv.at[1], send_sem=send_sem.at[8], recv_sem=recv_sem.at[8],
        device_id={"row": east}, device_id_type=MESH)
    to_west.start()
    to_east.start()

    lax.fori_loop(rows // 2 + 1, rows, send_back, 0)

    heat = jnp.zeros((8, cells), F32)
    prow = iota((8, total_rows), 0)
    plane = iota((8, total_rows), 1)
    hrow = iota((8, cells), 0)
    for k in range(kb):
        want = jnp.full((8, total_rows), -1, jnp.int32)
        for b in range(blocks // kb):
            want = jnp.where(prow == b, srcs[k, b], want)
        picked = dot(jnp.where(plane == want, 1.0, 0.0).astype(BF), sst).astype(BF)
        for b in range(blocks // kb):
            heat = heat + jnp.where(hrow == b, dot(picked, wts[b * kb + k]), 0.0)
    out_heat[...] = heat[0 : blocks // kb, :]

    to_west.wait()
    to_east.wait()
    from_east, from_west = ewrecv[0], ewrecv[1]
    sides = []
    for i in range(count):
        e_part = pltpu.roll(from_east, (cells - 4 * i) % cells, 1)
        w_part = pltpu.roll(from_west, 4 * i, 1)
        sides.append(jnp.where(lane24 < 4, e_part, jnp.where(lane24 >= cells - 4, w_part, 0.0)))
    ypos = iota((held, cells), 0)
    grow = comp * tile + jnp.where(ypos < tile + 4, ypos, ypos - held)
    grow = lax.rem(grow + total_rows, total_rows)
    up_open = (grow != 0).astype(F32)
    down_open = (grow != total_rows - 1).astype(F32)
    first_lane, last_lane = lane24 == 0, lane24 == cells - 1
    state = [(wide_slabs[i], sides[i]) for i in range(8)]
    kh = [(wide_slabs[8 + k], sides[8 + k]) for k in range(4)]
    for _ in range(NSTEP):
        new = []
        for t in range(2):
            for k in range(4):
                core, side = state[t * 4 + k]
                above = state[t * 4 + max(k - 1, 0)]
                below = state[t * 4 + min(k + 1, 3)]
                ce, se = pltpu.roll(core, cells - 1, 1), pltpu.roll(side, cells - 1, 1)
                cw, sw = pltpu.roll(core, 1, 1), pltpu.roll(side, 1, 1)
                easts = (jnp.where(last_lane, se, ce), jnp.where(last_lane, ce, se))
                wests = (jnp.where(first_lane, sw, cw), jnp.where(first_lane, cw, sw))
                pair = []
                for q in range(2):
                    v = state[t * 4 + k][q]
                    up = pltpu.roll(v, 1, 0)
                    down = pltpu.roll(v, held - 1, 0)
                    lateral = (up - v) * up_open + (down - v) * down_open + (easts[q] - v) + (wests[q] - v)
                    vertical = above[q] + below[q] - 2.0 * v
                    pair.append(v + kh[k][q] * lateral + kap_v[k] * vertical)
                new.append(tuple(pair))
        state = new
    for t in range(2):
        for k in range(4):
            out_ocean[t, k] = state[t * 4 + k][0][:tile]

    own2.wait()
    across.wait_send()
    wait_bytes(send2.at[pl.ds(0, rows - 1)], recv_sem.at[6])
    wait_bytes(send1.at[pl.ds(0, rows - 1)], send_sem.at[0])
    wait_bytes(send2.at[pl.ds(0, rows - 1)], send_sem.at[6])
    wait_bytes(gath.at[pl.ds(0, half - 1)], send_sem.at[2])
    wait_bytes(gath.at[pl.ds(0, half - 1)], send_sem.at[3])


def body(
    fourier,
    legendre,
    gauss_weight,
    kappa_spec,
    marine_tracer_fields,
    kappa_h,
    kappa_v,
    air_flux,
    remap_weight,
    remap_source,
):
    rows = lax.axis_size("row")
    comps = lax.axis_size("comp")
    hemis, waves, wide = fourier.shape
    nlat, ns = legendre.shape[1:]
    tracers, levels, tile, cells = marine_tracer_fields.shape
    blocks = remap_weight.shape[0] * remap_weight.shape[2]
    vm = pl.BlockSpec(memory_space=pltpu.VMEM)
    anyspace = pl.BlockSpec(memory_space=pl.ANY)
    spectral, ocean, heat = pl.pallas_call(
        kernel,
        out_shape=(
            jax.ShapeDtypeStruct((waves, 2, wide), BF),
            jax.ShapeDtypeStruct(marine_tracer_fields.shape, F32),
            jax.ShapeDtypeStruct((remap_weight.shape[0], cells), F32),
        ),
        in_specs=[anyspace] * 10,
        out_specs=(anyspace, vm, vm),
        scratch_shapes=[
            pltpu.VMEM(fourier.shape, BF),
            pltpu.VMEM((nlat, ns), BF),
            pltpu.SMEM(gauss_weight.shape, F32),
            pltpu.VMEM(kappa_spec.shape, BF),
            pltpu.VMEM(marine_tracer_fields.shape, F32),
            pltpu.VMEM(kappa_h.shape, F32),
            pltpu.SMEM(kappa_v.shape, F32),
            pltpu.VMEM(air_flux.shape, BF),
            pltpu.VMEM((blocks, cells, cells), BF),
            pltpu.SMEM(remap_source.shape[:1:-1] + remap_source.shape[:1], jnp.int32),
            pltpu.VMEM((nlat, ns), BF),
            pltpu.VMEM((waves, 2, wide), BF),
            pltpu.VMEM((waves, 2, wide), BF),
            pltpu.VMEM((waves, 2, wide), BF),
            pltpu.VMEM((comps, 48, cells), BF),
            pltpu.VMEM((2, 6, 8, cells), F32),
            pltpu.VMEM((2, 6, 8, cells), F32),
            pltpu.VMEM((2, tile + 8, cells), F32),
            pltpu.VMEM((2, tile + 8, cells), F32),
            pltpu.SemaphoreType.DMA((12,)),
            pltpu.SemaphoreType.DMA((9,)),
            pltpu.SemaphoreType.DMA((9,)),
            pltpu.SemaphoreType.REGULAR((rows,)),
            pltpu.SemaphoreType.REGULAR,
        ],
        compiler_params=pltpu.CompilerParams(
            collective_id=0, has_side_effects=True, vmem_limit_bytes=60 * 2**20
        ),
    )(
        fourier,
        legendre[0],
        gauss_weight,
        kappa_spec,
        marine_tracer_fields,
        kappa_h,
        kappa_v,
        air_flux,
        remap_weight.reshape(blocks, cells, cells),
        remap_source[:, 0, :].T,
    )
    spectral = spectral.reshape(waves, 2, hemis, wide // 2)
    spectral = jnp.transpose(spectral, (2, 0, 1, 3)).reshape(fourier.shape)
    return spectral, ocean, heat


def solution(mesh):
    return jax.shard_map(
        body,
        mesh=mesh,
        in_specs=(
            P(None, "comp", "row"),
            P(("comp", "row"), None, None),
            P(),
            P(),
            P(None, None, "comp", "row"),
            P(None, "comp", "row"),
            P(),
            P(None, "comp", "row"),
            P("comp", "row", None, None, None),
            P("comp", "row", None),
        ),
        out_specs=(P(None, "comp", "row"), P(None, None, "comp", "row"), P("comp", "row")),
        check_vma=False,
    )
```

```python
import functools

import jax
import jax.numpy as jnp
from jax import lax
from jax.experimental import pallas as pl
from jax.experimental.pallas import tpu as pltpu
from jax.sharding import PartitionSpec as P

NSTEP = 4
MESH = pl.DeviceIdType.MESH
BF = jnp.bfloat16
F32 = jnp.float32
NN = (((1,), (0,)), ((), ()))
NT = (((1,), (1,)), ((), ()))
TN = (((0,), (0,)), ((), ()))


def dot(a, b, dims=NN):
    return lax.dot_general(a, b, dims, preferred_element_type=F32)


def iota(shape, axis):
    return lax.broadcasted_iota(jnp.int32, shape, axis)


def wait_bytes(ref, sem):
    pltpu.make_async_copy(ref, ref, sem).wait()


def kernel(
    four_hbm, leg_hbm, gauss_hbm, kappa_hbm, fields_hbm, kap_h_hbm, kap_v_hbm, flux_hbm, wts_hbm, srcs_hbm,
    out_spec, out_ocean, out_heat,
    four, leg, gauss, kappa, fields, kap_h, kap_v, flux, wts, srcs,
    perm_leg, send1, recv1, send2, gath, nspack, nsrecv, ewpack, ewrecv,
    loc_sem, send_sem, recv_sem, ready, upper,
):
    rows = lax.axis_size("row")
    comps = lax.axis_size("comp")
    me = lax.axis_index("row")
    comp = lax.axis_index("comp")
    half = comps // 2
    zhi = comp // half
    inner = lax.rem(comp, half)
    partner = lax.rem(comp + half, comps)
    north = lax.rem(comp + comps - 1, comps)
    south = lax.rem(comp + 1, comps)
    west = lax.rem(me + rows - 1, rows)
    east = lax.rem(me + 1, rows)

    pairs = (
        (four_hbm, four), (gauss_hbm, gauss), (flux_hbm, flux), (srcs_hbm, srcs), (fields_hbm, fields), (wts_hbm, wts),
        (kap_h_hbm, kap_h), (kap_v_hbm, kap_v), (kappa_hbm, kappa), (leg_hbm, leg),
    )
    loads = [pltpu.make_async_copy(a, b, loc_sem.at[2 + i]) for i, (a, b) in enumerate(pairs)]
    for load in loads:
        load.start()

    ahead = 1 - 2 * zhi
    earlier = jnp.where(zhi == 0, me, rows - 1 - me)
    later = rows - 1 - earlier
    at_end = jnp.where((inner == 0) | (inner == half - 1), 1, 0)
    across_end = jnp.where(inner == 0, north, south)
    barrier = pltpu.get_barrier_semaphore()

    def greet_row(k, _):
        pl.semaphore_signal(barrier, inc=1, device_id={"row": me + ahead * k}, device_id_type=MESH)
        return 0

    def greet_comp(k, _):
        target = zhi * half + lax.rem(inner + k, half)
        pl.semaphore_signal(barrier, inc=1, device_id={"comp": target}, device_id_type=MESH)
        return 0

    lax.fori_loop(1, later + 1, greet_row, 0)
    lax.fori_loop(1, half, greet_comp, 0)

    @pl.when(zhi == 0)
    def _():
        pl.semaphore_signal(barrier, inc=1, device_id={"comp": partner}, device_id_type=MESH)

    @pl.when((zhi == 0) & (at_end == 1))
    def _():
        pl.semaphore_signal(barrier, inc=1, device_id={"comp": across_end}, device_id_type=MESH)

    wide = four.shape[2]
    cols = kappa.shape[0]
    lats = wide // cols
    mid = wide // 2
    lane_lat = iota((1, wide), 1) // cols
    loads[0].wait()
    loads[1].wait()
    weight = jnp.zeros((1, wide), F32)
    for l in range(lats):
        weight = jnp.where(lane_lat == l, gauss[me * lats + l], weight)
    n = four[0].astype(F32)
    s = four[1].astype(F32)
    even = (weight * (n + s)).astype(BF)
    odd = (weight * (n - s)).astype(BF)
    first = jnp.concatenate([even[:, :mid], odd[:, :mid]], axis=1)
    second = jnp.concatenate([even[:, mid:], odd[:, mid:]], axis=1)
    send1[:, 0, :] = first
    send1[:, 1, :] = second

    pl.semaphore_wait(barrier, earlier + half - 1 + zhi * (1 + at_end))

    def answer_row(k, _):
        pl.semaphore_signal(ready.at[me], inc=1, device_id={"row": me - ahead * k}, device_id_type=MESH)
        return 0

    lax.fori_loop(1, earlier + 1, answer_row, 0)

    @pl.when(zhi == 1)
    def _():
        pl.semaphore_signal(upper, inc=1, device_id={"comp": partner}, device_id_type=MESH)

    @pl.when((zhi == 1) & (at_end == 1))
    def _():
        pl.semaphore_signal(upper, inc=1, device_id={"comp": across_end}, device_id_type=MESH)

    def forward_to(target):
        pltpu.make_async_remote_copy(
            src_ref=send1.at[target], dst_ref=recv1.at[me], send_sem=send_sem.at[0], recv_sem=recv_sem.at[0],
            device_id={"row": target}, device_id_type=MESH).start()

    def forward_earlier(k, _):
        forward_to(me - ahead * (earlier + 1 - k))
        return 0

    lax.fori_loop(1, earlier + 1, forward_earlier, 0)
    own1 = pltpu.make_async_copy(send1.at[me], recv1.at[me], loc_sem.at[0])
    own1.start()

    for load in loads[2:6]:
        load.wait()
    tile = fields.shape[2]
    cells = fields.shape[3]
    blocks = wts.shape[0]
    kb = srcs.shape[0]
    row16 = iota((16, cells), 0)
    lane16 = iota((16, cells), 1)
    rep = jnp.zeros((16, cells), F32)
    for f in range(2):
        for j in range(blocks):
            rep = jnp.where(row16 == f * blocks + j, flux[f, j // kb, :].astype(F32)[None, :], rep)
    contrib = jnp.zeros((16, cells), F32)
    for j in range(blocks):
        only = jnp.where(lax.rem(row16, blocks) == j, rep, 0.0).astype(BF)
        contrib = contrib + dot(only, wts[j], NT)
    src_row = jnp.zeros((16, cells), F32)
    for j in range(blocks):
        hit = (lane16 // 16 == inner) & (lax.rem(lane16, blocks) == j) & (row16 == zhi)
        src_row = jnp.where(hit, srcs[j % kb, j // kb].astype(F32), src_row)
    gath[comp, 0:16, :] = fields[0, 0].astype(BF)
    gath[comp, 16:32, :] = contrib.astype(BF)
    gath[comp, 32:48, :] = src_row.astype(BF)
    across = pltpu.make_async_remote_copy(
        src_ref=gath.at[comp], dst_ref=gath.at[comp], send_sem=send_sem.at[1], recv_sem=recv_sem.at[1],
        device_id={"comp": partner}, device_id_type=MESH)

    @pl.when(zhi == 1)
    def _():
        across.start()

    def send_inner(slot, which):
        def step(k, _):
            target = zhi * half + lax.rem(inner + k, half)
            pltpu.make_async_remote_copy(
                src_ref=gath.at[slot], dst_ref=gath.at[slot], send_sem=send_sem.at[which], recv_sem=recv_sem.at[which],
                device_id={"comp": target}, device_id_type=MESH).start()
            return 0

        lax.fori_loop(1, half, step, 0)

    send_inner(comp, 2)

    loads[6].wait()
    slabs = [fields[t, k] for t in range(2) for k in range(4)] + [kap_h[k] for k in range(4)]
    count = len(slabs)
    row8 = iota((8, cells), 0)
    for p in range(count // 2):
        a, b = slabs[2 * p], slabs[2 * p + 1]
        nspack[0, p] = jnp.where(row8 < 4, a[:8], pltpu.roll(b[:8], 4, 0))
        nspack[1, p] = jnp.where(row8 >= 4, a[tile - 8 :], pltpu.roll(b[tile - 8 :], 4, 0))
    to_north = pltpu.make_async_remote_copy(
        src_ref=nspack.at[0], dst_ref=nsrecv.at[0], send_sem=send_sem.at[4], recv_sem=recv_sem.at[4],
        device_id={"comp": north}, device_id_type=MESH)
    to_south = pltpu.make_async_remote_copy(
        src_ref=nspack.at[1], dst_ref=nsrecv.at[1], send_sem=send_sem.at[5], recv_sem=recv_sem.at[5],
        device_id={"comp": south}, device_id_type=MESH)
    north_first = (zhi == 1) | (inner > 0)
    south_first = (zhi == 1) | (inner < half - 1)

    @pl.when(north_first)
    def _():
        to_north.start()

    @pl.when(south_first)
    def _():
        to_south.start()

    for load in loads[7:]:
        load.wait()
    nlat = leg.shape[0]
    group = 2 * rows
    gi = iota((256, 256), 0)
    pick = (iota((256, 256), 1) == 8 * lax.rem(gi, 32) + gi // 32).astype(F32).astype(BF)
    for b in range(nlat // 256):
        part = dot(pick, leg[b * 256 : (b + 1) * 256, :]).astype(BF)
        for l in range(8):
            perm_leg[l * group + b * 32 : l * group + b * 32 + 32, :] = part[l * 32 : (l + 1) * 32, :]

    def forward_later(k, _):
        target = me + ahead * k
        pl.semaphore_wait(ready.at[target], 1)
        forward_to(target)
        return 0

    lax.fori_loop(1, later + 1, forward_later, 0)

    own1.wait()
    wait_bytes(recv1.at[pl.ds(0, rows - 1)], recv_sem.at[0])
    data = recv1[...].reshape(group, wide)
    hw = perm_leg.shape[1] // 2
    top = float((comps * rows + 2 * hw - 1) * (comps * rows + 2 * hw))
    wave = comp * rows + me
    kappa_col = kappa[...].astype(F32).reshape(1, cols).T
    grids = []
    for h in range(2):
        x = jnp.concatenate(
            [data[:, h * mid + l * cols : h * mid + (l + 1) * cols] for l in range(8)], axis=0
        )
        ph = perm_leg[:, h * hw : (h + 1) * hw]
        spec = dot(x, ph, TN) / nlat
        degree = (2 * iota((1, hw), 1) + wave + h).astype(F32)
        ratio = degree * (degree + 1.0) / top
        factor = 1.0 / (1.0 + kappa_col * (ratio * ratio))
        filt = (spec * factor).astype(BF)
        grids.append(dot(ph, filt, NT))
    north_grid = (grids[0] + grids[1]).astype(BF)
    south_grid = (grids[0] - grids[1]).astype(BF)
    back = jnp.concatenate(
        [g[l * group : (l + 1) * group, :] for g in (north_grid, south_grid) for l in range(8)], axis=1
    )
    send2[...] = back.reshape(rows, 2, wide)

    @pl.when(zhi == 0)
    def _():
        pl.semaphore_wait(upper, 1 + at_end)
        across.start()

    @pl.when(jnp.logical_not(north_first))
    def _():
        to_north.start()

    @pl.when(jnp.logical_not(south_first))
    def _():
        to_south.start()

    across.wait_recv()
    send_inner(partner, 3)

    def send_back(k, _):
        step = (k + 1) // 2
        turn = jnp.where(lax.rem(k, 2) == 1, step, rows - step)
        target = lax.rem(me + turn, rows)
        pltpu.make_async_remote_copy(
            src_ref=send2.at[target], dst_ref=out_spec.at[me], send_sem=send_sem.at[6], recv_sem=recv_sem.at[6],
            device_id={"row": target}, device_id_type=MESH).start()
        return 0

    lax.fori_loop(1, rows // 2 + 1, send_back, 0)
    own2 = pltpu.make_async_copy(send2.at[me], out_spec.at[me], loc_sem.at[1])
    own2.start()

    wait_bytes(gath.at[pl.ds(0, half - 1)], recv_sem.at[2])
    wait_bytes(gath.at[pl.ds(0, half - 1)], recv_sem.at[3])
    total_rows = comps * tile
    held = tile + 8
    sst = gath[:, 0:16, :].reshape(total_rows, cells)
    contribs = gath[:, 16:32, :].reshape(comps * 16, cells)
    src16 = jnp.sum(gath[:, 32:48, :].astype(F32), axis=0).astype(jnp.int32)
    src = jnp.concatenate([src16[0:1, :], src16[1:2, :]], axis=1)
    pos = iota((2 * held, comps * 16), 0)
    pos_f = pos // held
    pos_y = pos - pos_f * held
    pos_y = jnp.where(pos_y < tile + 4, pos_y, pos_y - held)
    pos_y = lax.rem(comp * tile + pos_y + total_rows, total_rows)
    lane = iota((2 * held, comps * 16), 1)
    pick_f = (pos_y == src) & (lax.rem(lane // blocks, 2) == pos_f)
    forcing = dot(jnp.where(pick_f, 1.0, 0.0).astype(BF), contribs)

    to_north.wait()
    to_south.wait()
    wide_slabs = []
    for p in range(count // 2):
        from_south, from_north = nsrecv[0, p], nsrecv[1, p]
        halo_a = jnp.where(row8 < 4, from_south, from_north)
        halo_b = jnp.where(row8 < 4, pltpu.roll(from_south, 4, 0), pltpu.roll(from_north, 4, 0))
        wide_slabs.append(jnp.concatenate([slabs[2 * p], halo_a], axis=0))
        wide_slabs.append(jnp.concatenate([slabs[2 * p + 1], halo_b], axis=0))
    wide_slabs[0] = wide_slabs[0] + forcing[0:held]
    wide_slabs[4] = wide_slabs[4] + forcing[held:]

    lane24 = iota((held, cells), 1)
    westward = jnp.zeros((held, cells), F32)
    eastward = jnp.zeros((held, cells), F32)
    for i, slab in enumerate(wide_slabs):
        own_w = (lane24 >= 4 * i) & (lane24 < 4 * i + 4)
        own_e = (lane24 >= cells - 4 - 4 * i) & (lane24 < cells - 4 * i)
        westward = jnp.where(own_w, pltpu.roll(slab, 4 * i, 1), westward)
        eastward = jnp.where(own_e, pltpu.roll(slab, (cells - 4 * i) % cells, 1), eastward)
    ewpack[0] = westward
    ewpack[1] = eastward
    to_west = pltpu.make_async_remote_copy(
        src_ref=ewpack.at[0], dst_ref=ewrecv.at[0], send_sem=send_sem.at[7], recv_sem=recv_sem.at[7],
        device_id={"row": west}, device_id_type=MESH)
    to_east = pltpu.make_async_remote_copy(
        src_ref=ewpack.at[1], dst_ref=ewrecv.at[1], send_sem=send_sem.at[8], recv_sem=recv_sem.at[8],
        device_id={"row": east}, device_id_type=MESH)
    to_west.start()
    to_east.start()

    lax.fori_loop(rows // 2 + 1, rows, send_back, 0)

    heat = jnp.zeros((8, cells), F32)
    prow = iota((8, total_rows), 0)
    plane = iota((8, total_rows), 1)
    hrow = iota((8, cells), 0)
    for k in range(kb):
        want = jnp.full((8, total_rows), -1, jnp.int32)
        for b in range(blocks // kb):
            want = jnp.where(prow == b, srcs[k, b], want)
        picked = dot(jnp.where(plane == want, 1.0, 0.0).astype(BF), sst).astype(BF)
        for b in range(blocks // kb):
            heat = heat + jnp.where(hrow == b, dot(picked, wts[b * kb + k]), 0.0)
    out_heat[...] = heat[0 : blocks // kb, :]

    to_west.wait()
    to_east.wait()
    from_east, from_west = ewrecv[0], ewrecv[1]
    sides = []
    for i in range(count):
        e_part = pltpu.roll(from_east, (cells - 4 * i) % cells, 1)
        w_part = pltpu.roll(from_west, 4 * i, 1)
        sides.append(jnp.where(lane24 < 4, e_part, jnp.where(lane24 >= cells - 4, w_part, 0.0)))
    ypos = iota((held, cells), 0)
    grow = comp * tile + jnp.where(ypos < tile + 4, ypos, ypos - held)
    grow = lax.rem(grow + total_rows, total_rows)
    up_open = (grow != 0).astype(F32)
    down_open = (grow != total_rows - 1).astype(F32)
    first_lane, last_lane = lane24 == 0, lane24 == cells - 1
    state = [(wide_slabs[i], sides[i]) for i in range(8)]
    kh = [(wide_slabs[8 + k], sides[8 + k]) for k in range(4)]
    for _ in range(NSTEP):
        new = []
        for t in range(2):
            for k in range(4):
                core, side = state[t * 4 + k]
                above = state[t * 4 + max(k - 1, 0)]
                below = state[t * 4 + min(k + 1, 3)]
                ce, se = pltpu.roll(core, cells - 1, 1), pltpu.roll(side, cells - 1, 1)
                cw, sw = pltpu.roll(core, 1, 1), pltpu.roll(side, 1, 1)
                easts = (jnp.where(last_lane, se, ce), jnp.where(last_lane, ce, se))
                wests = (jnp.where(first_lane, sw, cw), jnp.where(first_lane, cw, sw))
                pair = []
                for q in range(2):
                    v = state[t * 4 + k][q]
                    up = pltpu.roll(v, 1, 0)
                    down = pltpu.roll(v, held - 1, 0)
                    lateral = (up - v) * up_open + (down - v) * down_open + (easts[q] - v) + (wests[q] - v)
                    vertical = above[q] + below[q] - 2.0 * v
                    pair.append(v + kh[k][q] * lateral + kap_v[k] * vertical)
                new.append(tuple(pair))
        state = new
    for t in range(2):
        for k in range(4):
            out_ocean[t, k] = state[t * 4 + k][0][:tile]

    own2.wait()
    across.wait_send()
    wait_bytes(send2.at[pl.ds(0, rows - 1)], recv_sem.at[6])
    wait_bytes(send1.at[pl.ds(0, rows - 1)], send_sem.at[0])
    wait_bytes(send2.at[pl.ds(0, rows - 1)], send_sem.at[6])
    wait_bytes(gath.at[pl.ds(0, half - 1)], send_sem.at[2])
    wait_bytes(gath.at[pl.ds(0, half - 1)], send_sem.at[3])


def arrange(spec_in, ocean_in, heat_in, spec_out, ocean_out, heat_out):
    mid = spec_in.shape[2] // 2
    for h in range(2):
        for u in range(2):
            spec_out[h, :, u * mid : (u + 1) * mid] = spec_in[:, u, h * mid : (h + 1) * mid]
    ocean_out[...] = ocean_in[...]
    heat_out[...] = heat_in[...]


def body(
    fourier,
    legendre,
    gauss_weight,
    kappa_spec,
    marine_tracer_fields,
    kappa_h,
    kappa_v,
    air_flux,
    remap_weight,
    remap_source,
):
    rows = lax.axis_size("row")
    comps = lax.axis_size("comp")
    hemis, waves, wide = fourier.shape
    nlat, ns = legendre.shape[1:]
    tracers, levels, tile, cells = marine_tracer_fields.shape
    blocks = remap_weight.shape[0] * remap_weight.shape[2]
    vm = pl.BlockSpec(memory_space=pltpu.VMEM)
    anyspace = pl.BlockSpec(memory_space=pl.ANY)
    spectral, ocean, heat = pl.pallas_call(
        kernel,
        out_shape=(
            jax.ShapeDtypeStruct((waves, 2, wide), BF),
            jax.ShapeDtypeStruct(marine_tracer_fields.shape, F32),
            jax.ShapeDtypeStruct((remap_weight.shape[0], cells), F32),
        ),
        in_specs=[anyspace] * 10,
        out_specs=(anyspace, vm, vm),
        scratch_shapes=[
            pltpu.VMEM(fourier.shape, BF),
            pltpu.VMEM((nlat, ns), BF),
            pltpu.SMEM(gauss_weight.shape, F32),
            pltpu.VMEM(kappa_spec.shape, BF),
            pltpu.VMEM(marine_tracer_fields.shape, F32),
            pltpu.VMEM(kappa_h.shape, F32),
            pltpu.SMEM(kappa_v.shape, F32),
            pltpu.VMEM(air_flux.shape, BF),
            pltpu.VMEM((blocks, cells, cells), BF),
            pltpu.SMEM(remap_source.shape[:1:-1] + remap_source.shape[:1], jnp.int32),
            pltpu.VMEM((nlat, ns), BF),
            pltpu.VMEM((waves, 2, wide), BF),
            pltpu.VMEM((waves, 2, wide), BF),
            pltpu.VMEM((waves, 2, wide), BF),
            pltpu.VMEM((comps, 48, cells), BF),
            pltpu.VMEM((2, 6, 8, cells), F32),
            pltpu.VMEM((2, 6, 8, cells), F32),
            pltpu.VMEM((2, tile + 8, cells), F32),
            pltpu.VMEM((2, tile + 8, cells), F32),
            pltpu.SemaphoreType.DMA((12,)),
            pltpu.SemaphoreType.DMA((9,)),
            pltpu.SemaphoreType.DMA((9,)),
            pltpu.SemaphoreType.REGULAR((rows,)),
            pltpu.SemaphoreType.REGULAR,
        ],
        compiler_params=pltpu.CompilerParams(
            collective_id=0, has_side_effects=True, vmem_limit_bytes=60 * 2**20
        ),
    )(
        fourier,
        legendre[0],
        gauss_weight,
        kappa_spec,
        marine_tracer_fields,
        kappa_h,
        kappa_v,
        air_flux,
        remap_weight.reshape(blocks, cells, cells),
        remap_source[:, 0, :].T,
    )
    return pl.pallas_call(
        arrange,
        out_shape=(
            jax.ShapeDtypeStruct(fourier.shape, BF),
            jax.ShapeDtypeStruct(ocean.shape, F32),
            jax.ShapeDtypeStruct(heat.shape, F32),
        ),
        in_specs=[vm, vm, vm],
        out_specs=(vm, vm, vm),
    )(spectral, ocean, heat)


def solution(mesh):
    return jax.shard_map(
        body,
        mesh=mesh,
        in_specs=(
            P(None, "comp", "row"),
            P(("comp", "row"), None, None),
            P(),
            P(),
            P(None, None, "comp", "row"),
            P(None, "comp", "row"),
            P(),
            P(None, "comp", "row"),
            P("comp", "row", None, None, None),
            P("comp", "row", None),
        ),
        out_specs=(P(None, "comp", "row"), P(None, None, "comp", "row"), P("comp", "row")),
        check_vma=False,
    )
```
